32 devices in a mesh: groups: 2 (over x), dp: 16 (over z, y, core).
Axes of the slice: x: 2, y: 2, z: 4, core: 2. Of those that a mesh axis runs over, the one named last changes fastest.
Arguments:
- acts: bfloat16 [4096, 8192], P(('groups', 'dp')), parts along dimension 0, may hold values from -6 to 6
- grads_out: bfloat16 [4096, 8192], P(('groups', 'dp')), parts along dimension 0, may hold values from -0.3984375 to 0.3984375
- tenant_ids: int32 [4096, 1], P(('groups', 'dp')), parts along dimension 0, may hold values from 0 to 7; in each aligned block of 128 rows (0 to 127, 128 to 255, ...) at most 32 rows name the same one
- owner: int32 [16], P('groups'), parts along dimension 0, may hold values from 0 to 7, each once
- a_half: float32 [32, 4096, 64], P(('groups', 'dp')), parts along dimension 0, may hold values from -0.0625 to 0.0625
- b_half: float32 [32, 64, 4096], P(('groups', 'dp')), parts along dimension 0, may hold values from -0.75 to 0.75
Outputs:
- input_grad: float32 [4096, 8192], P(('groups', 'dp')), parts along dimension 0
- grad_a: float32 [32, 4096, 64], P(('groups', 'dp')), parts along dimension 0
- grad_b: float32 [32, 64, 4096], P(('groups', 'dp')), parts along dimension 0
The draws below stay inside these ranges and needn't reach their ends.
There are 2 independent parts, one for each index of `groups`. The reference program is written for one: setup_inputs(seed, part) draws one part's arguments, and reference() takes and returns one part's arrays. A program takes and returns all parts, laid end to end along the dimension named above; each array names one. Nothing has to cross between parts.
Inputs may be any that keep to these rules, and one draw needn't show every extreme that they name: `tenant_ids`: one device's rows name each tenant at most 32 times. `owner`: each slot holds exactly one tenant.
All inputs are finite; a program needn't handle non-finite values.
Results may differ from the reference program's by a relative error of at most 0.0003.
Values may be sent and summed in bfloat16 or wider, within the bound.
A program may use at most 128 MiB of HBM per device.

```python
import math
import jax
import jax.numpy as jnp
import numpy as np
from jax import lax

D = 8192
R = 64
TOK_DEV = 128
TENANTS = 8
CAP = 32
TOKENS = 2048
N_DP = 16


def block_scale(key, shape, pieces, least, top_value):
    def one(axis_at, shards_of):
        steps = jax.random.uniform(jax.random.fold_in(jax.random.fold_in(key, 6), axis_at), (shards_of,), jnp.float32, least / len(pieces), top_value / len(pieces))
        return jnp.repeat(jnp.exp(steps), shape[axis_at] // shards_of).reshape((-1,) + (1,) * (len(shape) - axis_at - 1))

    gain = one(*pieces[0])
    for cut in pieces[1:]:
        gain = gain * one(*cut)
    return gain


def deal_out(stream_key, own, number, rows, count, top, most, slope):
    sequence = jax.random.permutation(stream_key, count)
    heavy_load, usual = load_shares(count, rows * top, most, slope, True), load_shares(count, rows * top, most, slope, False)
    places = jnp.arange(count)

    def named(tallies, turn):
        used = int((tallies > 0).sum())
        fixed = max(1, used // 4)
        moved = fixed + (places - fixed + turn * (used - fixed)) % max(1, count - fixed)
        return jnp.zeros((count,), jnp.int32).at[sequence[jnp.where(places < fixed, places, moved)]].set(jnp.asarray(tallies, jnp.int32))

    tallies = jnp.where(number % 4 == 0, named(heavy_load, number // 4), named(usual, number - number // 4 - 1))
    mixed = jax.random.permutation(jax.random.fold_in(own, 3), count)
    giver, sink = mixed[0:count // 2 * 2:2], mixed[1:count // 2 * 2:2]
    room = jnp.minimum(tallies[giver] - 1, most - tallies[sink]) // 2
    room = jnp.where((giver == sequence[0]) | (sink == sequence[0]) | (tallies[sink] == 0), 0, jnp.maximum(room, 0))
    moved = jax.random.randint(jax.random.fold_in(own, 4), (count // 2,), 0, 1 << 20) % (room + 1)
    tallies = tallies.at[giver].add(-moved).at[sink].add(moved)
    members = jnp.searchsorted(jnp.cumsum(tallies), jnp.arange(rows * top), side="right").astype(jnp.int32)
    grid = members.reshape(top, rows).T
    grid = grid[jax.random.permutation(jax.random.fold_in(own, 1), rows)]
    turn = jax.random.randint(jax.random.fold_in(own, 2), (rows, 1), 0, top)
    return jnp.take_along_axis(grid, (jnp.arange(top)[None, :] + turn) % top, axis=1)


def load_shares(count, total, most, slope, full):
    weights = [(1 << 20) // math.isqrt(rank ** slope) + 1 for rank in range(1, count + 1)]
    largest = most if full else min(most, max(-(-total // count), total * weights[0] // sum(weights)))
    least = 1 if total - largest >= count - 1 else 0
    holding, surplus = [largest] + [least] * (count - 1), total - largest - least * (count - 1)
    while surplus > 0:
        candidates = [i for i in range(1, count) if holding[i] < largest] or [i for i in range(1, count) if holding[i] < most]
        mass, budget = sum([weights[i] for i in candidates]), surplus
        for i in candidates:
            more = min(most - holding[i], max(1, budget * weights[i] // mass), surplus)
            holding[i] = holding[i] + more
            surplus = surplus - more
    return np.array(holding)


def noise(key, shape, deviation, bound, pieces=(), held_as=jnp.bfloat16):
    entries = deviation * jax.random.normal(key, shape, jnp.float32)
    if pieces:
        entries = entries * block_scale(key, shape, pieces, -0.22, 0.18)
    return jnp.clip(entries, -bound, bound).astype(held_as)


def setup_inputs(seed: int = 0, part: int = 0) -> dict:
    splits = jax.random.split(jax.random.key(seed), 7)
    part_keys = jax.random.split(jax.random.fold_in(splits[6], part), 7)
    acts = noise(part_keys[0], (TOKENS, D), 1.0, 6.0, ((0, 16),))
    grads_out = noise(part_keys[1], (TOKENS, D), 0.0625, 0.3984375, ((0, 16),))
    tenant_ids_keys = jax.random.split(jax.random.fold_in(part_keys[2], 1), TOKENS // TOK_DEV)
    tenant_ids_turns = jax.random.permutation(jax.random.fold_in(part_keys[2], 3), TOKENS // TOK_DEV)
    tenant_ids = jax.vmap(lambda own, number: deal_out(jax.random.fold_in(part_keys[2], 2), own, number, TOK_DEV, TENANTS, 1, CAP, 2))(tenant_ids_keys, tenant_ids_turns).reshape((TOKENS, 1))
    owner = jax.random.permutation(part_keys[3], TENANTS).astype(jnp.int32)
    a_half = noise(part_keys[4], (N_DP, D // 2, R), D ** -0.5, 0.0625, ((0, 16),), jnp.float32)
    b_half = noise(part_keys[5], (N_DP, R, D // 2), R ** -0.5, 0.75, ((0, 16),), jnp.float32)
    return {"acts": acts, "grads_out": grads_out, "tenant_ids": tenant_ids, "owner": owner, "a_half": a_half, "b_half": b_half}


def exact(left, right):
    return jnp.dot(left, right, precision=lax.Precision.HIGHEST, preferred_element_type=jnp.float32)


def reference(acts, grads_out, tenant_ids, owner, a_half, b_half):
    token_count, width = acts.shape
    tenants = owner.shape[0]
    half_width = width // 2
    rank = a_half.shape[2]
    a_full = a_half.reshape(tenants, width, rank)
    b_full = b_half.reshape(tenants, 2, rank, half_width).transpose(0, 2, 1, 3).reshape(tenants, rank, width)
    slot_row = owner[tenant_ids[:, 0]]
    limit = CAP * N_DP
    x_pad = jnp.concatenate([acts.astype(jnp.float32), jnp.zeros((1, width), jnp.float32)], axis=0)
    g_pad = jnp.concatenate([grads_out.astype(jnp.float32), jnp.zeros((1, width), jnp.float32)], axis=0)

    def step(carry, slot):
        picked = jnp.nonzero(slot_row == slot, size=limit, fill_value=token_count)[0].astype(jnp.int32)
        x_rows = x_pad[picked]
        g_rows = g_pad[picked]
        down = a_full[slot]
        upper = b_full[slot]
        low = exact(x_rows, down)
        back = exact(g_rows, upper.T)
        dx_rows = 2.0 * exact(back, down.T)
        carry = carry.at[picked].set(dx_rows)
        grad_down = 2.0 * exact(x_rows.T, back)
        grad_up = 2.0 * exact(low.T, g_rows)
        return carry, (grad_down, grad_up)

    start = jnp.zeros((token_count + 1, width), jnp.float32)
    input_grad, (grad_down, grad_up) = lax.scan(step, start, jnp.arange(tenants, dtype=jnp.int32))
    grad_a = grad_down.reshape(N_DP, half_width, rank)
    grad_b = grad_up.reshape(tenants, rank, 2, half_width).transpose(0, 2, 1, 3).reshape(N_DP, rank, half_width)
    return input_grad[:token_count], grad_a, grad_b
```

```python
import jax
import jax.numpy as jnp
from jax import lax
from jax.sharding import PartitionSpec as P


def from_partner(value, axis, stride):
    mask = 2**stride
    pairs = [(source, source ^ mask) for source in range(lax.axis_size(axis))]
    return lax.ppermute(value, axis, pairs)


def exact(left, right):
    return jnp.dot(left, right, precision=lax.Precision.HIGHEST, preferred_element_type=jnp.float32)


def placement(dest, slots):
    return (jnp.arange(slots, dtype=jnp.int32)[:, None] == dest[None, :]).astype(jnp.bfloat16)


def body(acts, grads_out, tenant_ids, owner, a_half, b_half):
    row_count, width = acts.shape
    group_size = lax.axis_size("dp")
    tenants = owner.shape[0]
    capacity = 4 * row_count // group_size
    half_width = width // 2
    first_half = lax.axis_index("dp") % 2 == 0
    onehot = (tenant_ids[:, 0][:, None] == jnp.arange(tenants, dtype=jnp.int32)[None, :]).astype(
        jnp.float32
    )
    row_iota = jnp.arange(row_count, dtype=jnp.int32)
    earlier = (row_iota[None, :] < row_iota[:, None]).astype(jnp.float32)
    before = jnp.dot(earlier, onehot, preferred_element_type=jnp.float32)
    rank_row = jnp.sum(before * onehot, axis=1).astype(jnp.int32)
    slot_row = jnp.sum(onehot * owner[None, :].astype(jnp.float32), axis=1).astype(jnp.int32)
    down_mine = a_half[0]
    up_mine = b_half[0]
    half_cap = capacity // 2
    slots = group_size * half_cap
    target = 2 * slot_row + rank_row % 2
    place = rank_row // 2
    route = placement(target * half_cap + place, slots)
    sent_x = (
        jnp.dot(route, acts, preferred_element_type=jnp.float32)
        .astype(jnp.bfloat16)
        .reshape(group_size, half_cap, width)
    )
    sent_g = (
        jnp.dot(route, grads_out, preferred_element_type=jnp.float32)
        .astype(jnp.bfloat16)
        .reshape(group_size, half_cap, width)
    )
    recv_x, recv_g = (
        lax.all_to_all(sent_x, "dp", split_axis=0, concat_axis=0, tiled=True),
        lax.all_to_all(sent_g, "dp", split_axis=0, concat_axis=0, tiled=True),
    )
    other_down, other_up = from_partner((down_mine, up_mine), "dp", 0)
    down_full = jnp.where(
        first_half,
        jnp.concatenate([down_mine, other_down], axis=0),
        jnp.concatenate([other_down, down_mine], axis=0),
    )
    up_full = jnp.where(
        first_half,
        jnp.concatenate([up_mine, other_up], axis=1),
        jnp.concatenate([other_up, up_mine], axis=1),
    )
    flat_x = recv_x.reshape(-1, width).astype(jnp.float32)
    flat_g = recv_g.reshape(-1, width).astype(jnp.float32)
    hidden_low = exact(flat_x, down_full)
    back_low = exact(flat_g, up_full.T)
    input_rows = 2.0 * exact(back_low, down_full.T)
    returned = lax.all_to_all(
        input_rows.reshape(group_size, half_cap, width),
        "dp",
        split_axis=0,
        concat_axis=0,
        tiled=True,
    )
    input_grad = exact(route.T.astype(jnp.float32), returned.reshape(slots, width))
    down_total = 2.0 * exact(flat_x.T, back_low)
    up_total = 2.0 * exact(hidden_low.T, flat_g)
    keep_down = jnp.where(first_half, down_total[:half_width], down_total[half_width:])
    give_down = jnp.where(first_half, down_total[half_width:], down_total[:half_width])
    keep_up = jnp.where(first_half, up_total[:, :half_width], up_total[:, half_width:])
    give_up = jnp.where(first_half, up_total[:, half_width:], up_total[:, :half_width])
    came_down, came_up = from_partner((give_down, give_up), "dp", 0)
    grad_down = keep_down + came_down
    grad_up = keep_up + came_up
    return (input_grad, grad_down[None], grad_up[None])


def split_bf16(value):
    high = lax.reduce_precision(value, exponent_bits=8, mantissa_bits=7)
    return high.astype(jnp.bfloat16), (value - high).astype(jnp.bfloat16)


def mm(left, right, dims):
    return lax.dot_general(left, right, (dims, ((), ())), preferred_element_type=jnp.float32)


def swap(value):
    return lax.all_to_all(value, "dp", split_axis=0, concat_axis=0, tiled=True)


BLOCK = 128
EXTRA = 16


def encode(value):
    chunks, rows, width = value.shape
    blocks = width // BLOCK
    cells = value.reshape(chunks, rows, blocks, BLOCK)
    peak = jnp.maximum(jnp.max(jnp.abs(cells), axis=3), 1e-30)
    power = jnp.ceil(jnp.log2(peak * (1.0 / 32000.0)))
    coded = jnp.round(cells * jnp.exp2(-power)[..., None]).astype(jnp.int16)
    coded = coded.reshape(chunks, rows, width)
    powers = power.astype(jnp.int16).reshape(chunks, -1)
    powers = jnp.pad(powers, ((0, 0), (0, EXTRA * width - powers.shape[1])))
    return jnp.concatenate([coded, powers.reshape(chunks, EXTRA, width)], axis=1)


def decode(coded, rows):
    chunks, _, width = coded.shape
    blocks = width // BLOCK
    powers = coded[:, rows:].reshape(chunks, EXTRA * width)[:, : rows * blocks]
    scale = jnp.exp2(powers.astype(jnp.float32)).reshape(chunks, rows, blocks, 1)
    cells = coded[:, :rows].astype(jnp.float32).reshape(chunks, rows, blocks, BLOCK)
    return (cells * scale).reshape(chunks, rows, width)


def by_columns(acts, grads_out, tenant_ids, owner, a_half, b_half):
    rows, width = acts.shape
    size = lax.axis_size("dp")
    slots = owner.shape[0]
    rank = a_half.shape[2]
    piece = width // (2 * size)
    chunk = 2 * piece
    total = rows * size
    hit = tenant_ids == jnp.arange(slots, dtype=jnp.int32)[None, :]
    slot_row = jnp.sum(jnp.where(hit, owner[None, :], 0), axis=1)
    slot_all = lax.all_gather(slot_row, "dp", tiled=True)
    mask = slot_all[None, :] == jnp.arange(slots, dtype=jnp.int32)[:, None]

    def adapters(value):
        sent = value.reshape(rank, size, piece).transpose(1, 0, 2)
        came = swap(sent).reshape(slots, 2, rank, piece).transpose(0, 2, 1, 3)
        return split_bf16(came.reshape(slots * rank, chunk))

    def tokens(value):
        sent = value.reshape(rows, 2, size, piece).transpose(2, 0, 1, 3)
        return swap(sent.reshape(size, rows, chunk)).reshape(total, chunk)

    def reduced(high, low, value):
        wide = mm(high, value, ((1,), (1,))) + mm(low, value, ((1,), (1,)))
        wide = wide.reshape(slots, rank, total)
        part = jnp.sum(jnp.where(mask[:, None, :], wide, 0.0), axis=0)
        part = part.reshape(rank, size, rows).transpose(1, 0, 2)
        mine = jnp.sum(swap(part), axis=0)
        whole = lax.all_gather(mine, "dp", axis=0).transpose(1, 0, 2).reshape(rank, total)
        expanded = jnp.where(mask[:, None, :], whole[None], 0.0).reshape(slots * rank, total)
        return split_bf16(expanded)

    up_high, up_low = adapters(b_half[0])
    grads = tokens(grads_out)
    back_high, back_low = reduced(up_high, up_low, grads)
    down_high, down_low = adapters(a_half[0].T)
    x = tokens(acts)
    low_high, low_low = reduced(down_high, down_low, x)
    dx = mm(back_high, down_high, ((0,), (0,)))
    dx = dx + (mm(back_low, down_high, ((0,), (0,))) + mm(back_high, down_low, ((0,), (0,))))
    coded = swap(encode((2.0 * dx).reshape(size, rows, chunk)))
    input_grad = decode(coded, rows).reshape(size, rows, 2, piece).transpose(1, 2, 0, 3)

    def returned(high, low, value):
        grad = 2.0 * (mm(high, value, ((1,), (0,))) + mm(low, value, ((1,), (0,))))
        sent = grad.reshape(slots, rank, 2, piece).transpose(0, 2, 1, 3)
        return swap(sent.reshape(size, rank, piece)).transpose(1, 0, 2).reshape(rank, size * piece)

    grad_down = returned(back_high, back_low, x)
    grad_up = returned(low_high, low_low, grads)
    return (input_grad.reshape(rows, width), grad_down.T[None], grad_up[None])


def solution(mesh):
    dp = mesh.shape["dp"]
    in_specs = (
        P(("groups", "dp"), None),
        P(("groups", "dp"), None),
        P(("groups", "dp"), None),
        P("groups"),
        P(("groups", "dp"), None, None),
        P(("groups", "dp"), None, None),
    )
    out_specs = (
        P(("groups", "dp"), None),
        P(("groups", "dp"), None, None),
        P(("groups", "dp"), None, None),
    )

    def choose(acts, *rest):
        narrow = acts.shape[1] // (2 * dp) >= BLOCK
        return (by_columns if narrow else body)(acts, *rest)

    return jax.shard_map(choose, mesh=mesh, in_specs=in_specs, out_specs=out_specs, check_vma=False)
```

```python
import functools

import jax
import jax.numpy as jnp
from jax import lax
from jax.experimental import pallas as pl
from jax.experimental.pallas import tpu as pltpu
from jax.sharding import PartitionSpec as P


def from_partner(value, axis, stride):
    mask = 2**stride
    pairs = [(source, source ^ mask) for source in range(lax.axis_size(axis))]
    return lax.ppermute(value, axis, pairs)


def exact(left, right):
    return jnp.dot(left, right, precision=lax.Precision.HIGHEST, preferred_element_type=jnp.float32)


def placement(dest, slots):
    return (jnp.arange(slots, dtype=jnp.int32)[:, None] == dest[None, :]).astype(jnp.bfloat16)


def body(acts, grads_out, tenant_ids, owner, a_half, b_half):
    row_count, width = acts.shape
    group_size = lax.axis_size("dp")
    tenants = owner.shape[0]
    capacity = 4 * row_count // group_size
    half_width = width // 2
    first_half = lax.axis_index("dp") % 2 == 0
    onehot = (tenant_ids[:, 0][:, None] == jnp.arange(tenants, dtype=jnp.int32)[None, :]).astype(
        jnp.float32
    )
    row_iota = jnp.arange(row_count, dtype=jnp.int32)
    earlier = (row_iota[None, :] < row_iota[:, None]).astype(jnp.float32)
    before = jnp.dot(earlier, onehot, preferred_element_type=jnp.float32)
    rank_row = jnp.sum(before * onehot, axis=1).astype(jnp.int32)
    slot_row = jnp.sum(onehot * owner[None, :].astype(jnp.float32), axis=1).astype(jnp.int32)
    down_mine = a_half[0]
    up_mine = b_half[0]
    half_cap = capacity // 2
    slots = group_size * half_cap
    target = 2 * slot_row + rank_row % 2
    place = rank_row // 2
    route = placement(target * half_cap + place, slots)
    sent_x = (
        jnp.dot(route, acts, preferred_element_type=jnp.float32)
        .astype(jnp.bfloat16)
        .reshape(group_size, half_cap, width)
    )
    sent_g = (
        jnp.dot(route, grads_out, preferred_element_type=jnp.float32)
        .astype(jnp.bfloat16)
        .reshape(group_size, half_cap, width)
    )
    recv_x, recv_g = (
        lax.all_to_all(sent_x, "dp", split_axis=0, concat_axis=0, tiled=True),
        lax.all_to_all(sent_g, "dp", split_axis=0, concat_axis=0, tiled=True),
    )
    other_down, other_up = from_partner((down_mine, up_mine), "dp", 0)
    down_full = jnp.where(
        first_half,
        jnp.concatenate([down_mine, other_down], axis=0),
        jnp.concatenate([other_down, down_mine], axis=0),
    )
    up_full = jnp.where(
        first_half,
        jnp.concatenate([up_mine, other_up], axis=1),
        jnp.concatenate([other_up, up_mine], axis=1),
    )
    flat_x = recv_x.reshape(-1, width).astype(jnp.float32)
    flat_g = recv_g.reshape(-1, width).astype(jnp.float32)
    hidden_low = exact(flat_x, down_full)
    back_low = exact(flat_g, up_full.T)
    input_rows = 2.0 * exact(back_low, down_full.T)
    returned = lax.all_to_all(
        input_rows.reshape(group_size, half_cap, width),
        "dp",
        split_axis=0,
        concat_axis=0,
        tiled=True,
    )
    input_grad = exact(route.T.astype(jnp.float32), returned.reshape(slots, width))
    down_total = 2.0 * exact(flat_x.T, back_low)
    up_total = 2.0 * exact(hidden_low.T, flat_g)
    keep_down = jnp.where(first_half, down_total[:half_width], down_total[half_width:])
    give_down = jnp.where(first_half, down_total[half_width:], down_total[:half_width])
    keep_up = jnp.where(first_half, up_total[:, :half_width], up_total[:, half_width:])
    give_up = jnp.where(first_half, up_total[:, half_width:], up_total[:, :half_width])
    came_down, came_up = from_partner((give_down, give_up), "dp", 0)
    grad_down = keep_down + came_down
    grad_up = keep_up + came_up
    return (input_grad, grad_down[None], grad_up[None])


def mm(left, right, dims):
    return lax.dot_general(left, right, (dims, ((), ())), preferred_element_type=jnp.float32)


MESH = pl.DeviceIdType.MESH


def kernel(
    size,
    slots,
    slot_mine,
    acts,
    grads_out,
    down,
    up,
    input_grad,
    grad_down,
    grad_up,
    slot_all,
    tok,
    adapt,
    weight,
    spread,
    part,
    red,
    full,
    coded,
    scale,
    coded_in,
    scale_in,
    acc,
    slot_send,
    slot_recv,
    tok_send,
    tok_recv,
    adapt_send,
    adapt_recv,
    part_send,
    part_recv,
    full_send,
    full_recv,
    dx_send,
    dx_recv,
    grad_send,
    grad_recv,
    local,
):
    me = lax.axis_index("dp")
    rows, width = acts.shape
    rank = down.shape[0]
    half = width // 2
    piece = half // size
    wide_rank = slots * rank
    tokens = (acts, grads_out)
    halves = (down, up)
    grads = (grad_down, grad_up)

    def peer(step):
        return lax.rem(me + step, size)

    def source(step):
        return lax.rem(me + size - step, size)

    def each(body_of):
        lax.fori_loop(1, size, lambda step, carry: (body_of(step), carry)[1], 0)

    def lanes(index, count):
        return pl.ds(pl.multiple_of(index * count, 128), count)

    def band(index, count):
        return pl.ds(pl.multiple_of(index * count, 64), count)

    def copy_to(src, dst, send, recv, dev):
        return pltpu.make_async_remote_copy(
            src_ref=src, dst_ref=dst, send_sem=send, recv_sem=recv,
            device_id={"dp": dev}, device_id_type=MESH,
        )

    def slot_copy(dev, at):
        return copy_to(slot_mine, slot_all.at[at], slot_send.at[dev], slot_recv.at[at], dev)

    def tok_copy(k, h, dev, at):
        return copy_to(
            tokens[k].at[:, pl.ds(pl.multiple_of(h * half + dev * piece, 128), piece)],
            tok.at[k, band(at, rows), pl.ds(h * piece, piece)],
            tok_send.at[k, dev, h], tok_recv.at[k, at, h], dev,
        )

    def adapt_place(k, at):
        return adapt.at[k, band(at // 2, rank), lanes(lax.rem(at, 2), piece)]

    def adapt_copy(k, dev, at):
        return copy_to(
            halves[k].at[:, lanes(dev, piece)], adapt_place(k, at),
            adapt_send.at[k, dev], adapt_recv.at[k, at], dev,
        )

    def part_copy(k, dev, at):
        return copy_to(
            part.at[k, dev], red.at[k, at], part_send.at[k, dev], part_recv.at[k, at], dev
        )

    def full_copy(k, dev, at, own):
        return copy_to(
            full.at[k, own], full.at[k, at], full_send.at[k, dev], full_recv.at[k, at], dev
        )

    def coded_copy(dev, at):
        return copy_to(coded.at[dev], coded_in.at[at], dx_send.at[0, dev], dx_recv.at[0, at], dev)

    def scale_copy(dev, at):
        return copy_to(scale.at[dev], scale_in.at[at], dx_send.at[1, dev], dx_recv.at[1, at], dev)

    def grad_piece(k, dev):
        return acc.at[k, band(dev // 2, rank), lanes(lax.rem(dev, 2), piece)]

    def grad_copy(k, dev, at):
        return copy_to(
            grad_piece(k, dev), grads[k].at[:, lanes(at, piece)],
            grad_send.at[k, dev], grad_recv.at[k, at], dev,
        )

    barrier = pltpu.get_barrier_semaphore()
    each(lambda step: pl.semaphore_signal(
        barrier, inc=1, device_id={"dp": peer(step)}, device_id_type=MESH))
    pl.semaphore_wait(barrier, size - 1)

    each(lambda step: slot_copy(peer(step), me).start())
    own = []
    for k in (1, 0):
        each(lambda step: adapt_copy(k, peer(step), me).start())

        def start_tokens(step):
            for h in range(2):
                tok_copy(k, h, peer(step), me).start()

        each(start_tokens)
        own.append(pltpu.make_async_copy(
            halves[k].at[:, lanes(me, piece)], adapt_place(k, me), local.at[k, 2]))
        for h in range(2):
            own.append(pltpu.make_async_copy(
                tokens[k].at[:, pl.ds(pl.multiple_of(h * half + me * piece, 128), piece)],
                tok.at[k, band(me, rows), pl.ds(h * piece, piece)], local.at[k, h]))
    for one in own:
        one.start()
    for one in own:
        one.wait()
    slot_all[me] = slot_mine[...]
    each(lambda step: slot_copy(peer(step), source(step)).wait_recv())

    def high_low(value):
        high = value.astype(jnp.bfloat16).astype(jnp.float32)
        return high, value - high

    def partial(k, at):
        wide = mm(weight[k], tok[k, band(at, rows), :], ((1,), (1,)))
        ids = slot_all[at][0:1, :]
        total = jnp.zeros((rank, rows), jnp.float32)
        for s in range(slots):
            value = wide[s * rank:(s + 1) * rank]
            value = value + wide[wide_rank + s * rank:wide_rank + (s + 1) * rank]
            total = total + jnp.where(ids == s, value, 0.0)
        return total

    def project(k):
        each(lambda step: adapt_copy(k, peer(step), source(step)).wait_recv())
        for s in range(slots):
            high, low = high_low(adapt[k, s * rank:(s + 1) * rank, :])
            weight[k, s * rank:(s + 1) * rank, :] = high.astype(jnp.bfloat16)
            weight[k, wide_rank + s * rank:wide_rank + (s + 1) * rank, :] = low.astype(jnp.bfloat16)
        red[k, me] = partial(k, me)

        def one(step):
            at = source(step)
            for h in range(2):
                tok_copy(k, h, peer(step), at).wait_recv()
            part[k, at] = partial(k, at)
            part_copy(k, at, me).start()

        each(one)

    def combine(k):
        each(lambda step: part_copy(k, peer(step), source(step)).wait_recv())
        full[k, me] = jnp.sum(red[k], axis=0)
        each(lambda step: full_copy(k, peer(step), me, me).start())

    def expand(k, at):
        ids = slot_all[at][0:1, :]
        high, low = high_low(full[k, at])
        for s in range(slots):
            spread[k, s * rank:(s + 1) * rank, lanes(at, rows)] = jnp.where(
                ids == s, high, 0.0).astype(jnp.bfloat16)
            spread[k, wide_rank + s * rank:wide_rank + (s + 1) * rank, lanes(at, rows)] = jnp.where(
                ids == s, low, 0.0).astype(jnp.bfloat16)

    project(1)
    combine(1)
    project(0)
    combine(0)

    def rows_grad(at, into, into_scale, dev):
        expand(1, at)
        high = spread[1, :wide_rank, lanes(at, rows)]
        low = spread[1, wide_rank:, lanes(at, rows)]
        dx = mm(high, weight[0, :wide_rank, :], ((0,), (0,)))
        dx = dx + mm(low, weight[0, :wide_rank, :], ((0,), (0,)))
        dx = 2.0 * (dx + mm(high, weight[0, wide_rank:, :], ((0,), (0,))))
        peak = jnp.maximum(jnp.max(jnp.abs(dx), axis=0, keepdims=True), 1e-30)
        value = jnp.floor(dx * (32700.0 / peak) + 0.5)
        into[dev] = value.astype(jnp.int32).astype(jnp.int16)
        unit = peak * (1.0 / 32700.0)
        for q in range(2 * piece // 128):
            into_scale[dev, q:q + 1, :] = unit[:, q * 128:(q + 1) * 128]

    rows_grad(me, coded_in, scale_in, me)

    def send_rows(step):
        at = source(step)
        full_copy(1, peer(step), at, me).wait_recv()
        rows_grad(at, coded, scale, at)
        coded_copy(at, me).start()
        scale_copy(at, me).start()

    each(send_rows)

    def weight_grad(k):
        def column(h, carry):
            value = mm(spread[1 - k], tok[k, :, lanes(h, piece)], ((1,), (0,)))
            acc[k, :, lanes(h, piece)] = 2.0 * (value[:wide_rank] + value[wide_rank:])
            return carry

        lax.fori_loop(0, 2, column, 0)
        grads[k][:, lanes(me, piece)] = grad_piece(k, me)[...]
        each(lambda step: grad_copy(k, peer(step), me).start())

    weight_grad(0)
    expand(0, me)

    def low_rows(step):
        at = source(step)
        full_copy(0, peer(step), at, me).wait_recv()
        expand(0, at)

    each(low_rows)
    weight_grad(1)

    def decode(at):
        for q in range(2 * piece // 128):
            h, r = divmod(q * 128, piece)
            value = coded_in[at, :, q * 128:(q + 1) * 128].astype(jnp.int32).astype(jnp.float32)
            start = pl.multiple_of(h * half + at * piece + r, 128)
            input_grad[:, pl.ds(start, 128)] = value * scale_in[at, q:q + 1, :]

    decode(me)

    def take(step):
        at = source(step)
        coded_copy(peer(step), at).wait_recv()
        scale_copy(peer(step), at).wait_recv()
        decode(at)

    each(take)

    def finish(step):
        dev, at = peer(step), source(step)
        for k in range(2):
            grad_copy(k, dev, at).wait_recv()
            grad_copy(k, dev, me).wait_send()
            for h in range(2):
                tok_copy(k, h, dev, me).wait_send()
            adapt_copy(k, dev, me).wait_send()
            part_copy(k, dev, me).wait_send()
            full_copy(k, dev, me, me).wait_send()
        slot_copy(dev, me).wait_send()
        coded_copy(dev, me).wait_send()
        scale_copy(dev, me).wait_send()

    each(finish)


def by_columns(acts, grads_out, tenant_ids, owner, a_half, b_half):
    rows, width = acts.shape
    size = lax.axis_size("dp")
    slots = owner.shape[0]
    rank = a_half.shape[2]
    chunk = width // size
    total = rows * size
    hit = tenant_ids == jnp.arange(slots, dtype=jnp.int32)[None, :]
    slot_row = jnp.sum(jnp.where(hit, owner[None, :], 0), axis=1)
    slot_mine = jnp.broadcast_to(slot_row[None, :], (8, rows))
    vmem = pl.BlockSpec(memory_space=pltpu.VMEM)
    hbm = pl.BlockSpec(memory_space=pl.ANY)
    dma = pltpu.SemaphoreType.DMA
    f32, bf16 = jnp.float32, jnp.bfloat16
    input_grad, grad_down, grad_up = pl.pallas_call(
        functools.partial(kernel, size, slots),
        out_shape=(
            jax.ShapeDtypeStruct((rows, width), f32),
            jax.ShapeDtypeStruct((rank, width // 2), f32),
            jax.ShapeDtypeStruct((rank, width // 2), f32),
        ),
        in_specs=[vmem, hbm, hbm, hbm, hbm],
        out_specs=(vmem, vmem, vmem),
        scratch_shapes=[
            pltpu.VMEM((size, 8, rows), jnp.int32),
            pltpu.VMEM((2, total, chunk), bf16),
            pltpu.VMEM((2, slots * rank, chunk), f32),
            pltpu.VMEM((2, 2 * slots * rank, chunk), bf16),
            pltpu.VMEM((2, 2 * slots * rank, total), bf16),
            pltpu.VMEM((2, size, rank, rows), f32),
            pltpu.VMEM((2, size, rank, rows), f32),
            pltpu.VMEM((2, size, rank, rows), f32),
            pltpu.VMEM((size, rows, chunk), jnp.int16),
            pltpu.VMEM((size, 8, 128), f32),
            pltpu.VMEM((size, rows, chunk), jnp.int16),
            pltpu.VMEM((size, 8, 128), f32),
            pltpu.VMEM((2, slots * rank, chunk), f32),
            dma((size,)), dma((size,)),
            dma((2, size, 2)), dma((2, size, 2)),
            dma((2, size)), dma((2, size)),
            dma((2, size)), dma((2, size)),
            dma((2, size)), dma((2, size)),
            dma((2, size)), dma((2, size)),
            dma((2, size)), dma((2, size)),
            dma((2, 3)),
        ],
        compiler_params=pltpu.CompilerParams(
            collective_id=0, has_side_effects=True, vmem_limit_bytes=56 * 2**20
        ),
        name="adapter_backward",
    )(slot_mine, acts, grads_out, a_half[0].T, b_half[0])
    return input_grad, grad_down.T[None], grad_up[None]


def solution(mesh):
    dp = mesh.shape["dp"]
    in_specs = (
        P(("groups", "dp"), None),
        P(("groups", "dp"), None),
        P(("groups", "dp"), None),
        P("groups"),
        P(("groups", "dp"), None, None),
        P(("groups", "dp"), None, None),
    )
    out_specs = (
        P(("groups", "dp"), None),
        P(("groups", "dp"), None, None),
        P(("groups", "dp"), None, None),
    )

    def choose(acts, *rest):
        narrow = acts.shape[1] // (2 * dp) % 128 == 0
        return (by_columns if narrow else body)(acts, *rest)

    return jax.shard_map(choose, mesh=mesh, in_specs=in_specs, out_specs=out_specs, check_vma=False)
```

```python
import functools

import jax
import jax.numpy as jnp
from jax import lax
from jax.experimental import pallas as pl
from jax.experimental.pallas import tpu as pltpu
from jax.sharding import PartitionSpec as P


def from_partner(value, axis, stride):
    mask = 2**stride
    pairs = [(source, source ^ mask) for source in range(lax.axis_size(axis))]
    return lax.ppermute(value, axis, pairs)


def exact(left, right):
    return jnp.dot(left, right, precision=lax.Precision.HIGHEST, preferred_element_type=jnp.float32)


def placement(dest, slots):
    return (jnp.arange(slots, dtype=jnp.int32)[:, None] == dest[None, :]).astype(jnp.bfloat16)


def body(acts, grads_out, tenant_ids, owner, a_half, b_half):
    row_count, width = acts.shape
    group_size = lax.axis_size("dp")
    tenants = owner.shape[0]
    capacity = 4 * row_count // group_size
    half_width = width // 2
    first_half = lax.axis_index("dp") % 2 == 0
    onehot = (tenant_ids[:, 0][:, None] == jnp.arange(tenants, dtype=jnp.int32)[None, :]).astype(
        jnp.float32
    )
    row_iota = jnp.arange(row_count, dtype=jnp.int32)
    earlier = (row_iota[None, :] < row_iota[:, None]).astype(jnp.float32)
    before = jnp.dot(earlier, onehot, preferred_element_type=jnp.float32)
    rank_row = jnp.sum(before * onehot, axis=1).astype(jnp.int32)
    slot_row = jnp.sum(onehot * owner[None, :].astype(jnp.float32), axis=1).astype(jnp.int32)
    down_mine = a_half[0]
    up_mine = b_half[0]
    half_cap = capacity // 2
    slots = group_size * half_cap
    target = 2 * slot_row + rank_row % 2
    place = rank_row // 2
    route = placement(target * half_cap + place, slots)
    sent_x = (
        jnp.dot(route, acts, preferred_element_type=jnp.float32)
        .astype(jnp.bfloat16)
        .reshape(group_size, half_cap, width)
    )
    sent_g = (
        jnp.dot(route, grads_out, preferred_element_type=jnp.float32)
        .astype(jnp.bfloat16)
        .reshape(group_size, half_cap, width)
    )
    recv_x, recv_g = (
        lax.all_to_all(sent_x, "dp", split_axis=0, concat_axis=0, tiled=True),
        lax.all_to_all(sent_g, "dp", split_axis=0, concat_axis=0, tiled=True),
    )
    other_down, other_up = from_partner((down_mine, up_mine), "dp", 0)
    down_full = jnp.where(
        first_half,
        jnp.concatenate([down_mine, other_down], axis=0),
        jnp.concatenate([other_down, down_mine], axis=0),
    )
    up_full = jnp.where(
        first_half,
        jnp.concatenate([up_mine, other_up], axis=1),
        jnp.concatenate([other_up, up_mine], axis=1),
    )
    flat_x = recv_x.reshape(-1, width).astype(jnp.float32)
    flat_g = recv_g.reshape(-1, width).astype(jnp.float32)
    hidden_low = exact(flat_x, down_full)
    back_low = exact(flat_g, up_full.T)
    input_rows = 2.0 * exact(back_low, down_full.T)
    returned = lax.all_to_all(
        input_rows.reshape(group_size, half_cap, width),
        "dp",
        split_axis=0,
        concat_axis=0,
        tiled=True,
    )
    input_grad = exact(route.T.astype(jnp.float32), returned.reshape(slots, width))
    down_total = 2.0 * exact(flat_x.T, back_low)
    up_total = 2.0 * exact(hidden_low.T, flat_g)
    keep_down = jnp.where(first_half, down_total[:half_width], down_total[half_width:])
    give_down = jnp.where(first_half, down_total[half_width:], down_total[:half_width])
    keep_up = jnp.where(first_half, up_total[:, :half_width], up_total[:, half_width:])
    give_up = jnp.where(first_half, up_total[:, half_width:], up_total[:, :half_width])
    came_down, came_up = from_partner((give_down, give_up), "dp", 0)
    grad_down = keep_down + came_down
    grad_up = keep_up + came_up
    return (input_grad, grad_down[None], grad_up[None])


def mm(left, right, dims):
    return lax.dot_general(left, right, (dims, ((), ())), preferred_element_type=jnp.float32)


MESH = pl.DeviceIdType.MESH


def kernel(
    size,
    slots,
    slot_mine,
    acts,
    grads_out,
    down,
    up,
    input_grad,
    grad_down,
    grad_up,
    slot_all,
    tok,
    adapt,
    weight,
    spread,
    part,
    red,
    full,
    coded,
    scale,
    coded_in,
    scale_in,
    ad_out,
    ad_scale,
    ad_scale_in,
    gr_out,
    gr_scale,
    gr_in,
    gr_scale_in,
    mid,
    mid_in,
    slot_send,
    slot_recv,
    tok_send,
    tok_recv,
    adapt_send,
    adapt_recv,
    ad_scale_send,
    ad_scale_recv,
    part_send,
    part_recv,
    full_send,
    full_recv,
    mid_send,
    mid_recv,
    dx_send,
    dx_recv,
    grad_send,
    grad_recv,
    local,
):
    me = lax.axis_index("dp")
    rows, width = acts.shape
    rank = down.shape[0]
    half = width // 2
    piece = half // size
    wide_rank = slots * rank
    tokens = (acts, grads_out)
    halves = (down, up)
    grads = (grad_down, grad_up)
    inner = size // 2
    base = (me // inner) * inner
    spot = me - base
    across = lax.rem(me + inner, size)
    quarters = piece // 128

    def peer(step):
        return lax.rem(me + step, size)

    def source(step):
        return lax.rem(me + size - step, size)

    def each(body_of):
        lax.fori_loop(1, size, lambda step, carry: (body_of(step), carry)[1], 0)

    def near(step):
        return lax.rem(spot + step, inner)

    def near_source(step):
        return lax.rem(spot + inner - step, inner)

    def each_near(body_of):
        lax.fori_loop(1, inner, lambda step, carry: (body_of(step), carry)[1], 0)

    def code(value):
        peak = jnp.maximum(jnp.max(jnp.abs(value), axis=0, keepdims=True), 1e-30)
        whole = jnp.floor(value * (32700.0 / peak) + 0.5).astype(jnp.int32).astype(jnp.int16)
        return whole, peak * (1.0 / 32700.0)

    def plain(value, unit):
        return value.astype(jnp.int32).astype(jnp.float32) * unit

    def lanes(index, count):
        return pl.ds(pl.multiple_of(index * count, 128), count)

    def band(index, count):
        return pl.ds(pl.multiple_of(index * count, 64), count)

    def copy_to(src, dst, send, recv, dev):
        return pltpu.make_async_remote_copy(
            src_ref=src, dst_ref=dst, send_sem=send, recv_sem=recv,
            device_id={"dp": dev}, device_id_type=MESH,
        )

    def slot_copy(dev, at):
        return copy_to(slot_mine, slot_all.at[at], slot_send.at[dev], slot_recv.at[at], dev)

    def tok_copy(k, h, dev, at):
        return copy_to(
            tokens[k].at[:, pl.ds(pl.multiple_of(h * half + dev * piece, 128), piece)],
            tok.at[k, band(at, rows), pl.ds(h * piece, piece)],
            tok_send.at[k, dev, h], tok_recv.at[k, at, h], dev,
        )

    def adapt_place(k, at):
        return adapt.at[k, band(at // 2, rank), lanes(lax.rem(at, 2), piece)]

    def adapt_copy(k, dev, at):
        return copy_to(
            ad_out.at[k, :, lanes(dev, piece)], adapt_place(k, at),
            adapt_send.at[k, dev], adapt_recv.at[k, at], dev,
        )

    def ad_scale_copy(dev, at):
        return copy_to(
            ad_scale.at[dev], ad_scale_in.at[at], ad_scale_send.at[dev], ad_scale_recv.at[at], dev
        )

    def part_copy(k, side, to, at):
        return copy_to(
            part.at[k, to, side], red.at[k, at, side],
            part_send.at[k, to, side], part_recv.at[k, at, side], base + to,
        )

    def mid_copy(k):
        return copy_to(mid.at[k], mid_in.at[k], mid_send.at[k], mid_recv.at[k], across)

    def full_copy(k, to, at):
        return copy_to(
            full.at[k, at], full.at[k, at], full_send.at[k, to], full_recv.at[k, at], base + to
        )

    def coded_copy(dev, at):
        return copy_to(coded.at[dev], coded_in.at[at], dx_send.at[0, dev], dx_recv.at[0, at], dev)

    def scale_copy(dev, at):
        return copy_to(scale.at[dev], scale_in.at[at], dx_send.at[1, dev], dx_recv.at[1, at], dev)

    def grad_copy(k, dev, at):
        return copy_to(
            gr_out.at[k, dev], gr_in.at[k, at], grad_send.at[0, k, dev], grad_recv.at[0, k, at], dev
        )

    def grad_scale_copy(k, dev, at):
        return copy_to(
            gr_scale.at[k, dev], gr_scale_in.at[k, at],
            grad_send.at[1, k, dev], grad_recv.at[1, k, at], dev,
        )

    barrier = pltpu.get_barrier_semaphore()
    each(lambda step: pl.semaphore_signal(
        barrier, inc=1, device_id={"dp": peer(step)}, device_id_type=MESH))
    pl.semaphore_wait(barrier, size - 1)

    each(lambda step: slot_copy(peer(step), me).start())
    own = []

    def start_tokens(k):
        def one(step):
            for h in range(2):
                tok_copy(k, h, peer(step), me).start()

        each(one)
        for h in range(2):
            copy = pltpu.make_async_copy(
                tokens[k].at[:, pl.ds(pl.multiple_of(h * half + me * piece, 128), piece)],
                tok.at[k, band(me, rows), pl.ds(h * piece, piece)], local.at[k, h])
            copy.start()
            own.append(copy)

    start_tokens(1)

    def code_adapters(dev, carry):
        for k in range(2):
            whole, unit = code(halves[k][:, lanes(dev, piece)])
            ad_out[k, :, lanes(dev, piece)] = whole
            for q in range(quarters):
                row = k * quarters + q
                ad_scale[dev, row:row + 1, :] = unit[:, q * 128:(q + 1) * 128]
        return carry

    lax.fori_loop(0, size, code_adapters, 0)

    def start_adapters(step):
        ad_scale_copy(peer(step), me).start()
        for k in (1, 0):
            adapt_copy(k, peer(step), me).start()

    each(start_adapters)
    start_tokens(0)
    for k in range(2):
        adapt_place(k, me)[...] = ad_out[k, :, lanes(me, piece)]
    ad_scale_in[me] = ad_scale[me]
    for one in own:
        one.wait()
    slot_all[me] = slot_mine[...]
    each(lambda step: slot_copy(peer(step), source(step)).wait_recv())

    def high_low(value):
        high = value.astype(jnp.bfloat16).astype(jnp.float32)
        return high, value - high

    def partial(k, at):
        wide = mm(weight[k], tok[k, band(at, rows), :], ((1,), (1,)))
        ids = slot_all[at][0:1, :]
        total = jnp.zeros((rank, rows), jnp.float32)
        for s in range(slots):
            value = wide[s * rank:(s + 1) * rank]
            value = value + wide[wide_rank + s * rank:wide_rank + (s + 1) * rank]
            total = total + jnp.where(ids == s, value, 0.0)
        return total

    def project(k):
        each(lambda step: adapt_copy(k, peer(step), source(step)).wait_recv())
        for s in range(slots):
            for q in range(2 * quarters):
                h, p = divmod(q, quarters)
                span = slice(q * 128, (q + 1) * 128)
                row = k * quarters + p
                high, low = high_low(plain(
                    adapt[k, s * rank:(s + 1) * rank, span], ad_scale_in[2 * s + h, row:row + 1, :]))
                weight[k, s * rank:(s + 1) * rank, span] = high.astype(jnp.bfloat16)
                weight[k, wide_rank + s * rank:wide_rank + (s + 1) * rank, span] = low.astype(
                    jnp.bfloat16)
        red[k, spot, me // inner] = partial(k, me)

        def one(step):
            at = source(step)
            for h in range(2):
                tok_copy(k, h, peer(step), at).wait_recv()
            value = partial(k, at)
            to, side = lax.rem(at, inner), at // inner

            @pl.when(step == inner)
            def _():
                red[k, spot, side] = value

            @pl.when(step != inner)
            def _():
                part[k, to, side] = value
                part_copy(k, side, to, spot).start()

        each(one)

    def meet(k):
        def one(step):
            for side in range(2):
                part_copy(k, side, near(step), near_source(step)).wait_recv()

        each_near(one)
        mid[k] = jnp.sum(red[k], axis=0)
        mid_copy(k).start()

    def tell(k):
        mid_copy(k).wait_recv()
        full[k, spot] = mid[k] + mid_in[k]
        each_near(lambda step: full_copy(k, near(step), spot).start())

    def hear(k):
        each_near(lambda step: full_copy(k, near(step), near_source(step)).wait_recv())

    def expand(k, at):
        ids = slot_all[at][0:1, :]
        high, low = high_low(full[k, lax.rem(at, inner), at // inner])
        for s in range(slots):
            spread[k, s * rank:(s + 1) * rank, lanes(at, rows)] = jnp.where(
                ids == s, high, 0.0).astype(jnp.bfloat16)
            spread[k, wide_rank + s * rank:wide_rank + (s + 1) * rank, lanes(at, rows)] = jnp.where(
                ids == s, low, 0.0).astype(jnp.bfloat16)

    each(lambda step: ad_scale_copy(peer(step), source(step)).wait_recv())
    project(1)
    meet(1)
    tell(1)
    project(0)
    meet(0)
    hear(1)

    def rows_grad(at, into, into_scale, dev):
        expand(1, at)
        high = spread[1, :wide_rank, lanes(at, rows)]
        low = spread[1, wide_rank:, lanes(at, rows)]
        dx = mm(high, weight[0, :wide_rank, :], ((0,), (0,)))
        dx = dx + mm(low, weight[0, :wide_rank, :], ((0,), (0,)))
        dx = 2.0 * (dx + mm(high, weight[0, wide_rank:, :], ((0,), (0,))))
        into[dev], unit = code(dx)
        for q in range(2 * piece // 128):
            into_scale[dev, q:q + 1, :] = unit[:, q * 128:(q + 1) * 128]

    rows_grad(me, coded_in, scale_in, me)

    def send_rows(step):
        at = source(step)
        rows_grad(at, coded, scale, at)
        coded_copy(at, me).start()
        scale_copy(at, me).start()

    each(send_rows)

    def weight_grad(k):
        def column(h, carry):
            value = mm(spread[1 - k], tok[k, :, lanes(h, piece)], ((1,), (0,)))
            value = 2.0 * (value[:wide_rank] + value[wide_rank:])
            for s in range(slots):
                whole, unit = code(value[s * rank:(s + 1) * rank])
                gr_out[k, 2 * s + h] = whole
                for q in range(quarters):
                    gr_scale[k, 2 * s + h, q:q + 1, :] = unit[:, q * 128:(q + 1) * 128]
            return carry

        lax.fori_loop(0, 2, column, 0)
        gr_in[k, me] = gr_out[k, me]
        gr_scale_in[k, me] = gr_scale[k, me]

        def send(step):
            grad_copy(k, peer(step), me).start()
            grad_scale_copy(k, peer(step), me).start()

        each(send)

    weight_grad(0)
    tell(0)
    hear(0)
    expand(0, me)
    each(lambda step: expand(0, source(step)))
    weight_grad(1)

    def decode_grad(k, at):
        for q in range(quarters):
            start = pl.multiple_of(at * piece + q * 128, 128)
            grads[k][:, pl.ds(start, 128)] = plain(
                gr_in[k, at, :, q * 128:(q + 1) * 128], gr_scale_in[k, at, q:q + 1, :])

    def decode(at):
        for q in range(2 * piece // 128):
            h, r = divmod(q * 128, piece)
            value = coded_in[at, :, q * 128:(q + 1) * 128]
            start = pl.multiple_of(h * half + at * piece + r, 128)
            input_grad[:, pl.ds(start, 128)] = plain(value, scale_in[at, q:q + 1, :])

    decode(me)

    def take(step):
        at = source(step)
        coded_copy(peer(step), at).wait_recv()
        scale_copy(peer(step), at).wait_recv()
        decode(at)

    each(take)

    def take_grad(k):
        decode_grad(k, me)

        def one(step):
            at = source(step)
            grad_copy(k, peer(step), at).wait_recv()
            grad_scale_copy(k, peer(step), at).wait_recv()
            decode_grad(k, at)

        each(one)

    take_grad(0)
    take_grad(1)

    def finish(step):
        dev = peer(step)
        for k in range(2):
            grad_copy(k, dev, me).wait_send()
            grad_scale_copy(k, dev, me).wait_send()
            for h in range(2):
                tok_copy(k, h, dev, me).wait_send()
            adapt_copy(k, dev, me).wait_send()
        slot_copy(dev, me).wait_send()
        ad_scale_copy(dev, me).wait_send()
        coded_copy(dev, me).wait_send()
        scale_copy(dev, me).wait_send()

    each(finish)

    def finish_near(step):
        for k in range(2):
            for side in range(2):
                part_copy(k, side, near(step), spot).wait_send()
            full_copy(k, near(step), spot).wait_send()

    each_near(finish_near)
    for k in range(2):
        mid_copy(k).wait_send()


def by_columns(acts, grads_out, tenant_ids, owner, a_half, b_half):
    rows, width = acts.shape
    size = lax.axis_size("dp")
    slots = owner.shape[0]
    rank = a_half.shape[2]
    chunk = width // size
    total = rows * size
    hit = tenant_ids == jnp.arange(slots, dtype=jnp.int32)[None, :]
    slot_row = jnp.sum(jnp.where(hit, owner[None, :], 0), axis=1)
    slot_mine = jnp.broadcast_to(slot_row[None, :], (8, rows))
    vmem = pl.BlockSpec(memory_space=pltpu.VMEM)
    hbm = pl.BlockSpec(memory_space=pl.ANY)
    dma = pltpu.SemaphoreType.DMA
    f32, bf16 = jnp.float32, jnp.bfloat16
    input_grad, grad_down, grad_up = pl.pallas_call(
        functools.partial(kernel, size, slots),
        out_shape=(
            jax.ShapeDtypeStruct((rows, width), f32),
            jax.ShapeDtypeStruct((rank, width // 2), f32),
            jax.ShapeDtypeStruct((rank, width // 2), f32),
        ),
        in_specs=[vmem, hbm, hbm, vmem, vmem],
        out_specs=(vmem, vmem, vmem),
        scratch_shapes=[
            pltpu.VMEM((size, 8, rows), jnp.int32),
            pltpu.VMEM((2, total, chunk), bf16),
            pltpu.VMEM((2, slots * rank, chunk), jnp.int16),
            pltpu.VMEM((2, 2 * slots * rank, chunk), bf16),
            pltpu.VMEM((2, 2 * slots * rank, total), bf16),
            pltpu.VMEM((2, size // 2, 2, rank, rows), f32),
            pltpu.VMEM((2, size // 2, 2, rank, rows), f32),
            pltpu.VMEM((2, size // 2, 2, rank, rows), f32),
            pltpu.VMEM((size, rows, chunk), jnp.int16),
            pltpu.VMEM((size, 8, 128), f32),
            pltpu.VMEM((size, rows, chunk), jnp.int16),
            pltpu.VMEM((size, 8, 128), f32),
            pltpu.VMEM((2, rank, width // 2), jnp.int16),
            pltpu.VMEM((size, 8, 128), f32),
            pltpu.VMEM((size, 8, 128), f32),
            pltpu.VMEM((2, size, rank, chunk // 2), jnp.int16),
            pltpu.VMEM((2, size, 8, 128), f32),
            pltpu.VMEM((2, size, rank, chunk // 2), jnp.int16),
            pltpu.VMEM((2, size, 8, 128), f32),
            pltpu.VMEM((2, 2, rank, rows), f32),
            pltpu.VMEM((2, 2, rank, rows), f32),
            dma((size,)), dma((size,)),
            dma((2, size, 2)), dma((2, size, 2)),
            dma((2, size)), dma((2, size)),
            dma((size,)), dma((size,)),
            dma((2, size // 2, 2)), dma((2, size // 2, 2)),
            dma((2, size // 2)), dma((2, size // 2)),
            dma((2,)), dma((2,)),
            dma((2, size)), dma((2, size)),
            dma((2, 2, size)), dma((2, 2, size)),
            dma((2, 2)),
        ],
        compiler_params=pltpu.CompilerParams(
            collective_id=0, has_side_effects=True, vmem_limit_bytes=56 * 2**20
        ),
        name="adapter_backward",
    )(slot_mine, acts, grads_out, a_half[0].T, b_half[0])
    return input_grad, grad_down.T[None], grad_up[None]


def solution(mesh):
    dp = mesh.shape["dp"]
    in_specs = (
        P(("groups", "dp"), None),
        P(("groups", "dp"), None),
        P(("groups", "dp"), None),
        P("groups"),
        P(("groups", "dp"), None, None),
        P(("groups", "dp"), None, None),
    )
    out_specs = (
        P(("groups", "dp"), None),
        P(("groups", "dp"), None, None),
        P(("groups", "dp"), None, None),
    )

    def choose(acts, *rest):
        narrow = acts.shape[1] // (2 * dp) % 128 == 0
        return (by_columns if narrow else body)(acts, *rest)

    return jax.shard_map(choose, mesh=mesh, in_specs=in_specs, out_specs=out_specs, check_vma=False)
```

```python
import functools

import jax
import jax.numpy as jnp
from jax import lax
from jax.experimental import pallas as pl
from jax.experimental.pallas import tpu as pltpu
from jax.sharding import PartitionSpec as P


def from_partner(value, axis, stride):
    mask = 2**stride
    pairs = [(source, source ^ mask) for source in range(lax.axis_size(axis))]
    return lax.ppermute(value, axis, pairs)


def exact(left, right):
    return jnp.dot(left, right, precision=lax.Precision.HIGHEST, preferred_element_type=jnp.float32)


def placement(dest, slots):
    return (jnp.arange(slots, dtype=jnp.int32)[:, None] == dest[None, :]).astype(jnp.bfloat16)


def body(acts, grads_out, tenant_ids, owner, a_half, b_half):
    row_count, width = acts.shape
    group_size = lax.axis_size("dp")
    tenants = owner.shape[0]
    capacity = 4 * row_count // group_size
    half_width = width // 2
    first_half = lax.axis_index("dp") % 2 == 0
    onehot = (tenant_ids[:, 0][:, None] == jnp.arange(tenants, dtype=jnp.int32)[None, :]).astype(
        jnp.float32
    )
    row_iota = jnp.arange(row_count, dtype=jnp.int32)
    earlier = (row_iota[None, :] < row_iota[:, None]).astype(jnp.float32)
    before = jnp.dot(earlier, onehot, preferred_element_type=jnp.float32)
    rank_row = jnp.sum(before * onehot, axis=1).astype(jnp.int32)
    slot_row = jnp.sum(onehot * owner[None, :].astype(jnp.float32), axis=1).astype(jnp.int32)
    down_mine = a_half[0]
    up_mine = b_half[0]
    half_cap = capacity // 2
    slots = group_size * half_cap
    target = 2 * slot_row + rank_row % 2
    place = rank_row // 2
    route = placement(target * half_cap + place, slots)
    sent_x = (
        jnp.dot(route, acts, preferred_element_type=jnp.float32)
        .astype(jnp.bfloat16)
        .reshape(group_size, half_cap, width)
    )
    sent_g = (
        jnp.dot(route, grads_out, preferred_element_type=jnp.float32)
        .astype(jnp.bfloat16)
        .reshape(group_size, half_cap, width)
    )
    recv_x, recv_g = (
        lax.all_to_all(sent_x, "dp", split_axis=0, concat_axis=0, tiled=True),
        lax.all_to_all(sent_g, "dp", split_axis=0, concat_axis=0, tiled=True),
    )
    other_down, other_up = from_partner((down_mine, up_mine), "dp", 0)
    down_full = jnp.where(
        first_half,
        jnp.concatenate([down_mine, other_down], axis=0),
        jnp.concatenate([other_down, down_mine], axis=0),
    )
    up_full = jnp.where(
        first_half,
        jnp.concatenate([up_mine, other_up], axis=1),
        jnp.concatenate([other_up, up_mine], axis=1),
    )
    flat_x = recv_x.reshape(-1, width).astype(jnp.float32)
    flat_g = recv_g.reshape(-1, width).astype(jnp.float32)
    hidden_low = exact(flat_x, down_full)
    back_low = exact(flat_g, up_full.T)
    input_rows = 2.0 * exact(back_low, down_full.T)
    returned = lax.all_to_all(
        input_rows.reshape(group_size, half_cap, width),
        "dp",
        split_axis=0,
        concat_axis=0,
        tiled=True,
    )
    input_grad = exact(route.T.astype(jnp.float32), returned.reshape(slots, width))
    down_total = 2.0 * exact(flat_x.T, back_low)
    up_total = 2.0 * exact(hidden_low.T, flat_g)
    keep_down = jnp.where(first_half, down_total[:half_width], down_total[half_width:])
    give_down = jnp.where(first_half, down_total[half_width:], down_total[:half_width])
    keep_up = jnp.where(first_half, up_total[:, :half_width], up_total[:, half_width:])
    give_up = jnp.where(first_half, up_total[:, half_width:], up_total[:, :half_width])
    came_down, came_up = from_partner((give_down, give_up), "dp", 0)
    grad_down = keep_down + came_down
    grad_up = keep_up + came_up
    return (input_grad, grad_down[None], grad_up[None])


def mm(left, right, dims):
    return lax.dot_general(left, right, (dims, ((), ())), preferred_element_type=jnp.float32)


MESH = pl.DeviceIdType.MESH


def kernel(
    size,
    slots,
    slot_mine,
    acts,
    grads_out,
    down,
    up,
    coded_in,
    scale_in,
    grad_down,
    grad_up,
    slot_all,
    tok,
    adapt,
    weight,
    spread,
    part,
    red,
    full,
    coded,
    scale,
    ad_out,
    ad_scale,
    ad_scale_in,
    gr_out,
    gr_scale,
    gr_in,
    gr_scale_in,
    mid,
    mid_in,
    slot_send,
    slot_recv,
    tok_send,
    tok_recv,
    adapt_send,
    adapt_recv,
    ad_scale_send,
    ad_scale_recv,
    part_send,
    part_recv,
    full_send,
    full_recv,
    mid_send,
    mid_recv,
    dx_send,
    dx_recv,
    grad_send,
    grad_recv,
    local,
):
    me = lax.axis_index("dp")
    rows, width = acts.shape
    rank = down.shape[0]
    half = width // 2
    piece = half // size
    wide_rank = slots * rank
    tokens = (acts, grads_out)
    halves = (down, up)
    grads = (grad_down, grad_up)
    inner = size // 2
    base = (me // inner) * inner
    spot = me - base
    across = lax.rem(me + inner, size)
    quarters = piece // 128

    def peer(step):
        return lax.rem(me + step, size)

    def source(step):
        return lax.rem(me + size - step, size)

    def each(body_of):
        lax.fori_loop(1, size, lambda step, carry: (body_of(step), carry)[1], 0)

    def near(step):
        return lax.rem(spot + step, inner)

    def near_source(step):
        return lax.rem(spot + inner - step, inner)

    def each_near(body_of):
        lax.fori_loop(1, inner, lambda step, carry: (body_of(step), carry)[1], 0)

    def code(value):
        peak = jnp.maximum(jnp.max(jnp.abs(value), axis=0, keepdims=True), 1e-30)
        whole = jnp.floor(value * (32700.0 / peak) + 0.5).astype(jnp.int32).astype(jnp.int16)
        return whole, peak * (1.0 / 32700.0)

    def plain(value, unit):
        return value.astype(jnp.int32).astype(jnp.float32) * unit

    def lanes(index, count):
        return pl.ds(pl.multiple_of(index * count, 128), count)

    def band(index, count):
        return pl.ds(pl.multiple_of(index * count, 64), count)

    def copy_to(src, dst, send, recv, dev):
        return pltpu.make_async_remote_copy(
            src_ref=src, dst_ref=dst, send_sem=send, recv_sem=recv,
            device_id={"dp": dev}, device_id_type=MESH,
        )

    def slot_copy(dev, at):
        return copy_to(slot_mine, slot_all.at[at], slot_send.at[dev], slot_recv.at[at], dev)

    def tok_copy(k, h, dev, at):
        return copy_to(
            tokens[k].at[:, pl.ds(pl.multiple_of(h * half + dev * piece, 128), piece)],
            tok.at[k, band(at, rows), pl.ds(h * piece, piece)],
            tok_send.at[k, dev, h], tok_recv.at[k, at, h], dev,
        )

    def adapt_place(k, at):
        return adapt.at[k, band(at // 2, rank), lanes(lax.rem(at, 2), piece)]

    def adapt_copy(k, dev, at):
        return copy_to(
            ad_out.at[k, :, lanes(dev, piece)], adapt_place(k, at),
            adapt_send.at[k, dev], adapt_recv.at[k, at], dev,
        )

    def ad_scale_copy(dev, at):
        return copy_to(
            ad_scale.at[dev], ad_scale_in.at[at], ad_scale_send.at[dev], ad_scale_recv.at[at], dev
        )

    def part_copy(k, side, to, at):
        return copy_to(
            part.at[k, to, side], red.at[k, at, side],
            part_send.at[k, to, side], part_recv.at[k, at, side], base + to,
        )

    def mid_copy(k):
        return copy_to(mid.at[k], mid_in.at[k], mid_send.at[k], mid_recv.at[k], across)

    def full_copy(k, to, at):
        return copy_to(
            full.at[k, at], full.at[k, at], full_send.at[k, to], full_recv.at[k, at], base + to
        )

    def coded_copy(dev, at):
        return copy_to(coded.at[dev], coded_in.at[at], dx_send.at[0, dev], dx_recv.at[0, at], dev)

    def scale_copy(dev, at):
        return copy_to(scale.at[dev], scale_in.at[at], dx_send.at[1, dev], dx_recv.at[1, at], dev)

    def grad_copy(k, dev, at):
        return copy_to(
            gr_out.at[k, dev], gr_in.at[k, at], grad_send.at[0, k, dev], grad_recv.at[0, k, at], dev
        )

    def grad_scale_copy(k, dev, at):
        return copy_to(
            gr_scale.at[k, dev], gr_scale_in.at[k, at],
            grad_send.at[1, k, dev], grad_recv.at[1, k, at], dev,
        )

    barrier = pltpu.get_barrier_semaphore()
    each(lambda step: pl.semaphore_signal(
        barrier, inc=1, device_id={"dp": peer(step)}, device_id_type=MESH))
    pl.semaphore_wait(barrier, size - 1)

    each(lambda step: slot_copy(peer(step), me).start())
    own = []

    def start_tokens(k):
        def one(step):
            for h in range(2):
                tok_copy(k, h, peer(step), me).start()

        each(one)
        for h in range(2):
            copy = pltpu.make_async_copy(
                tokens[k].at[:, pl.ds(pl.multiple_of(h * half + me * piece, 128), piece)],
                tok.at[k, band(me, rows), pl.ds(h * piece, piece)], local.at[k, h])
            copy.start()
            own.append(copy)

    start_tokens(1)

    def code_adapters(dev, carry):
        for k in range(2):
            whole, unit = code(halves[k][:, lanes(dev, piece)])
            ad_out[k, :, lanes(dev, piece)] = whole
            for q in range(quarters):
                row = k * quarters + q
                ad_scale[dev, row:row + 1, :] = unit[:, q * 128:(q + 1) * 128]
        return carry

    lax.fori_loop(0, size, code_adapters, 0)

    def start_adapters(step):
        ad_scale_copy(peer(step), me).start()
        for k in (1, 0):
            adapt_copy(k, peer(step), me).start()

    each(start_adapters)
    start_tokens(0)
    for k in range(2):
        adapt_place(k, me)[...] = ad_out[k, :, lanes(me, piece)]
    ad_scale_in[me] = ad_scale[me]
    for one in own:
        one.wait()
    slot_all[me] = slot_mine[...]
    each(lambda step: slot_copy(peer(step), source(step)).wait_recv())

    def high_low(value):
        high = value.astype(jnp.bfloat16).astype(jnp.float32)
        return high, value - high

    def partial(k, at):
        wide = mm(weight[k], tok[k, band(at, rows), :], ((1,), (1,)))
        ids = slot_all[at][0:1, :]
        total = jnp.zeros((rank, rows), jnp.float32)
        for s in range(slots):
            value = wide[s * rank:(s + 1) * rank]
            value = value + wide[wide_rank + s * rank:wide_rank + (s + 1) * rank]
            total = total + jnp.where(ids == s, value, 0.0)
        return total

    def project(k):
        each(lambda step: adapt_copy(k, peer(step), source(step)).wait_recv())
        for s in range(slots):
            for q in range(2 * quarters):
                h, p = divmod(q, quarters)
                span = slice(q * 128, (q + 1) * 128)
                row = k * quarters + p
                high, low = high_low(plain(
                    adapt[k, s * rank:(s + 1) * rank, span], ad_scale_in[2 * s + h, row:row + 1, :]))
                weight[k, s * rank:(s + 1) * rank, span] = high.astype(jnp.bfloat16)
                weight[k, wide_rank + s * rank:wide_rank + (s + 1) * rank, span] = low.astype(
                    jnp.bfloat16)
        red[k, spot, me // inner] = partial(k, me)

        def one(step):
            at = source(step)
            for h in range(2):
                tok_copy(k, h, peer(step), at).wait_recv()
            value = partial(k, at)
            to, side = lax.rem(at, inner), at // inner

            @pl.when(step == inner)
            def _():
                red[k, spot, side] = value

            @pl.when(step != inner)
            def _():
                part[k, to, side] = value
                part_copy(k, side, to, spot).start()

        each(one)

    def meet(k):
        def one(step):
            for side in range(2):
                part_copy(k, side, near(step), near_source(step)).wait_recv()

        each_near(one)
        mid[k] = jnp.sum(red[k], axis=0)
        mid_copy(k).start()

    def tell(k):
        mid_copy(k).wait_recv()
        full[k, spot] = mid[k] + mid_in[k]
        each_near(lambda step: full_copy(k, near(step), spot).start())

    def hear(k):
        each_near(lambda step: full_copy(k, near(step), near_source(step)).wait_recv())

    def expand(k, at):
        ids = slot_all[at][0:1, :]
        high, low = high_low(full[k, lax.rem(at, inner), at // inner])
        for s in range(slots):
            spread[k, s * rank:(s + 1) * rank, lanes(at, rows)] = jnp.where(
                ids == s, high, 0.0).astype(jnp.bfloat16)
            spread[k, wide_rank + s * rank:wide_rank + (s + 1) * rank, lanes(at, rows)] = jnp.where(
                ids == s, low, 0.0).astype(jnp.bfloat16)

    each(lambda step: ad_scale_copy(peer(step), source(step)).wait_recv())
    project(1)
    meet(1)
    tell(1)
    project(0)
    meet(0)
    hear(1)

    def rows_grad(at, into, into_scale, dev):
        expand(1, at)
        high = spread[1, :wide_rank, lanes(at, rows)]
        low = spread[1, wide_rank:, lanes(at, rows)]
        dx = mm(high, weight[0, :wide_rank, :], ((0,), (0,)))
        dx = dx + mm(low, weight[0, :wide_rank, :], ((0,), (0,)))
        dx = 2.0 * (dx + mm(high, weight[0, wide_rank:, :], ((0,), (0,))))
        into[dev], unit = code(dx)
        for q in range(2 * piece // 128):
            into_scale[dev, q:q + 1, :] = unit[:, q * 128:(q + 1) * 128]

    rows_grad(me, coded_in, scale_in, me)

    def send_rows(step):
        at = source(step)
        rows_grad(at, coded, scale, at)
        coded_copy(at, me).start()
        scale_copy(at, me).start()

    each(send_rows)

    def weight_grad(k):
        def column(h, carry):
            value = mm(spread[1 - k], tok[k, :, lanes(h, piece)], ((1,), (0,)))
            value = 2.0 * (value[:wide_rank] + value[wide_rank:])
            for s in range(slots):
                whole, unit = code(value[s * rank:(s + 1) * rank])
                gr_out[k, 2 * s + h] = whole
                for q in range(quarters):
                    gr_scale[k, 2 * s + h, q:q + 1, :] = unit[:, q * 128:(q + 1) * 128]
            return carry

        lax.fori_loop(0, 2, column, 0)
        gr_in[k, me] = gr_out[k, me]
        gr_scale_in[k, me] = gr_scale[k, me]

        def send(step):
            grad_copy(k, peer(step), me).start()
            grad_scale_copy(k, peer(step), me).start()

        each(send)

    weight_grad(0)
    tell(0)
    hear(0)
    expand(0, me)
    each(lambda step: expand(0, source(step)))
    weight_grad(1)

    def decode_grad(k, at):
        for q in range(quarters):
            start = pl.multiple_of(at * piece + q * 128, 128)
            grads[k][:, pl.ds(start, 128)] = plain(
                gr_in[k, at, :, q * 128:(q + 1) * 128], gr_scale_in[k, at, q:q + 1, :])


    def take(step):
        at = source(step)
        coded_copy(peer(step), at).wait_recv()
        scale_copy(peer(step), at).wait_recv()

    each(take)

    def take_grad(k):
        decode_grad(k, me)

        def one(step):
            at = source(step)
            grad_copy(k, peer(step), at).wait_recv()
            grad_scale_copy(k, peer(step), at).wait_recv()
            decode_grad(k, at)

        each(one)

    take_grad(0)
    take_grad(1)

    def finish(step):
        dev = peer(step)
        for k in range(2):
            grad_copy(k, dev, me).wait_send()
            grad_scale_copy(k, dev, me).wait_send()
            for h in range(2):
                tok_copy(k, h, dev, me).wait_send()
            adapt_copy(k, dev, me).wait_send()
        slot_copy(dev, me).wait_send()
        ad_scale_copy(dev, me).wait_send()
        coded_copy(dev, me).wait_send()
        scale_copy(dev, me).wait_send()

    each(finish)

    def finish_near(step):
        for k in range(2):
            for side in range(2):
                part_copy(k, side, near(step), spot).wait_send()
            full_copy(k, near(step), spot).wait_send()

    each_near(finish_near)
    for k in range(2):
        mid_copy(k).wait_send()


def by_columns(acts, grads_out, tenant_ids, owner, a_half, b_half):
    rows, width = acts.shape
    size = lax.axis_size("dp")
    slots = owner.shape[0]
    rank = a_half.shape[2]
    chunk = width // size
    total = rows * size
    hit = tenant_ids == jnp.arange(slots, dtype=jnp.int32)[None, :]
    slot_row = jnp.sum(jnp.where(hit, owner[None, :], 0), axis=1)
    slot_mine = jnp.broadcast_to(slot_row[None, :], (8, rows))
    vmem = pl.BlockSpec(memory_space=pltpu.VMEM)
    hbm = pl.BlockSpec(memory_space=pl.ANY)
    dma = pltpu.SemaphoreType.DMA
    f32, bf16 = jnp.float32, jnp.bfloat16
    coded, scale, grad_down, grad_up = pl.pallas_call(
        functools.partial(kernel, size, slots),
        out_shape=(
            jax.ShapeDtypeStruct((size, rows, chunk), jnp.int16),
            jax.ShapeDtypeStruct((size, 8, 128), f32),
            jax.ShapeDtypeStruct((rank, width // 2), f32),
            jax.ShapeDtypeStruct((rank, width // 2), f32),
        ),
        in_specs=[vmem, hbm, hbm, vmem, vmem],
        out_specs=(vmem, vmem, vmem, vmem),
        scratch_shapes=[
            pltpu.VMEM((size, 8, rows), jnp.int32),
            pltpu.VMEM((2, total, chunk), bf16),
            pltpu.VMEM((2, slots * rank, chunk), jnp.int16),
            pltpu.VMEM((2, 2 * slots * rank, chunk), bf16),
            pltpu.VMEM((2, 2 * slots * rank, total), bf16),
            pltpu.VMEM((2, size // 2, 2, rank, rows), f32),
            pltpu.VMEM((2, size // 2, 2, rank, rows), f32),
            pltpu.VMEM((2, size // 2, 2, rank, rows), f32),
            pltpu.VMEM((size, rows, chunk), jnp.int16),
            pltpu.VMEM((size, 8, 128), f32),
            pltpu.VMEM((2, rank, width // 2), jnp.int16),
            pltpu.VMEM((size, 8, 128), f32),
            pltpu.VMEM((size, 8, 128), f32),
            pltpu.VMEM((2, size, rank, chunk // 2), jnp.int16),
            pltpu.VMEM((2, size, 8, 128), f32),
            pltpu.VMEM((2, size, rank, chunk // 2), jnp.int16),
            pltpu.VMEM((2, size, 8, 128), f32),
            pltpu.VMEM((2, 2, rank, rows), f32),
            pltpu.VMEM((2, 2, rank, rows), f32),
            dma((size,)), dma((size,)),
            dma((2, size, 2)), dma((2, size, 2)),
            dma((2, size)), dma((2, size)),
            dma((size,)), dma((size,)),
            dma((2, size // 2, 2)), dma((2, size // 2, 2)),
            dma((2, size // 2)), dma((2, size // 2)),
            dma((2,)), dma((2,)),
            dma((2, size)), dma((2, size)),
            dma((2, 2, size)), dma((2, 2, size)),
            dma((2, 2)),
        ],
        compiler_params=pltpu.CompilerParams(
            collective_id=0, has_side_effects=True, vmem_limit_bytes=56 * 2**20
        ),
        name="adapter_backward",
    )(slot_mine, acts, grads_out, a_half[0].T, b_half[0])
    unit = scale[:, :chunk // 128].reshape(size, 1, chunk)
    input_grad = coded.astype(f32) * unit
    input_grad = input_grad.reshape(size, rows, 2, chunk // 2).transpose(1, 2, 0, 3)
    input_grad = input_grad.reshape(rows, width)
    return input_grad, grad_down.T[None], grad_up[None]


def solution(mesh):
    dp = mesh.shape["dp"]
    in_specs = (
        P(("groups", "dp"), None),
        P(("groups", "dp"), None),
        P(("groups", "dp"), None),
        P("groups"),
        P(("groups", "dp"), None, None),
        P(("groups", "dp"), None, None),
    )
    out_specs = (
        P(("groups", "dp"), None),
        P(("groups", "dp"), None, None),
        P(("groups", "dp"), None, None),
    )

    def choose(acts, *rest):
        narrow = acts.shape[1] // (2 * dp) % 128 == 0
        return (by_columns if narrow else body)(acts, *rest)

    return jax.shard_map(choose, mesh=mesh, in_specs=in_specs, out_specs=out_specs, check_vma=False)
```
